512 devices in a mesh: row: 32 (over x, z), col: 16 (over y, core).
Axes of the slice: x: 4, y: 8, z: 8, core: 2. Of those that a mesh axis runs over, the one named last changes fastest.
Arguments:
- features: bfloat16 [65536, 128], P(('row', 'col')), may hold values from -6 to 6
- weight: bfloat16 [128, 256], replicated, may hold values from -0.5 to 0.5
- edge_tiles: bfloat16 [32, 16, 144, 128, 128], P('row', 'col'), may hold values from -0.046875 to 0.046875
- tile_row: int32 [32, 16, 144], P('row', 'col'), may hold values from 0 to 15
- tile_col: int32 [32, 16, 144], P('row', 'col'), may hold values from 0 to 31
- tile_count: int32 [32, 16], P('row', 'col'), may hold values from 36 to 144, as said below
- labels: int32 [65536], P(('row', 'col')), may hold values from -40 to 171
- cotangent: bfloat16 [65536, 256], P(('row', 'col')), may hold values from -6 to 6
Outputs:
- activation: bfloat16 [65536, 256], P(('row', 'col'))
- grad_features: bfloat16 [65536, 128], P(('row', 'col'))
- grad_weight: float32 [128, 256], replicated
The draws below stay inside these ranges and needn't reach their ends.
Inputs may be any that keep to these rules, and one draw needn't show every extreme that they name: Slots 0 to tile_count[r, c] - 1 of grid block (r, c) are live and the later ones are ignored; tile positions may repeat within a block, and repeated tiles add.
All inputs are finite; a program needn't handle non-finite values.
Results may differ from the reference program's by a relative error of at most 0.029.
Values may be sent and summed in bfloat16 or wider, within the bound.
A program may use at most 64 MiB of HBM per device.

```python
import jax
import jax.numpy as jnp
from jax import lax

F_IN = 128
HIDDEN_SIZE = 256
TILE = 128
NODE_DEV = 128
TPD = 144
NODES = 65536
RB = 16
CB = 32
N_ROW = 32
N_COL = 16


def draw_tile_count(key, part):
    key = jax.random.fold_in(key, 7)
    first_key, second_key = jax.random.split(key)
    places = N_ROW * N_COL
    tallies = jax.random.randint(first_key, (places,), TPD // 4, TPD + 1)
    chosen = jax.random.randint(second_key, (), 0, places)
    tallies = tallies.at[chosen].set(TPD)
    tallies = tallies.at[(chosen + 1) % places].set(TPD // 4)
    return tallies.reshape(N_ROW, N_COL).astype(jnp.int32)


def touch_ends(drawn, rng, low, largest):
    place = [jax.random.randint(jax.random.fold_in(rng, axis), (), 0, length) for axis, length in enumerate(drawn.shape)]
    longest = drawn.shape.index(max(drawn.shape))
    next_to = place[:longest] + [(place[longest] + 1) % drawn.shape[longest]] + place[longest + 1:]
    return drawn.at[tuple(place)].set(low).at[tuple(next_to)].set(largest)


def level_of(key, dims, shards, smallest, high):
    def one(dim, shards_of):
        steps = jax.random.uniform(jax.random.fold_in(jax.random.fold_in(key, 6), dim), (shards_of,), jnp.float32, smallest / len(shards), high / len(shards))
        return jnp.repeat(jnp.exp(steps), dims[dim] // shards_of).reshape((-1,) + (1,) * (len(dims) - dim - 1))

    factor_of = one(*shards[0])
    for cut in shards[1:]:
        factor_of = factor_of * one(*cut)
    return factor_of


def noise(key, extent, scale, bound, shards=(), kind=jnp.bfloat16):
    result = scale * jax.random.normal(key, extent, jnp.float32)
    if shards:
        result = result * level_of(key, extent, shards, -0.22, 0.18)
    return jnp.clip(result, -bound, bound).astype(kind)


def setup_inputs(seed: int = 0) -> dict:
    keys = jax.random.split(jax.random.key(seed), 9)
    return {
        "features": noise(keys[0], (NODES, F_IN), 1.0, 6.0, ((0, 512),)),
        "weight": noise(keys[1], (F_IN, HIDDEN_SIZE), F_IN ** -0.5, 0.5),
        "edge_tiles": noise(keys[2], (N_ROW, N_COL, TPD, TILE, TILE), (TPD * TILE * TILE // NODE_DEV) ** -0.5, 0.046875, ((0, 32), (1, 16))),
        "tile_row": touch_ends(jax.random.randint(keys[3], (N_ROW, N_COL, TPD), 0, RB), jax.random.fold_in(keys[3], 1), 0, RB - 1).astype(jnp.int32),
        "tile_col": touch_ends(jax.random.randint(keys[4], (N_ROW, N_COL, TPD), 0, CB), jax.random.fold_in(keys[4], 1), 0, CB - 1).astype(jnp.int32),
        "tile_count": draw_tile_count(jax.random.fold_in(keys[8], 71), 0),
        "labels": touch_ends(jax.random.randint(keys[6], (NODES,), -40, 172), jax.random.fold_in(keys[6], 1), -40, 171).astype(jnp.int32),
        "cotangent": noise(keys[7], (NODES, HIDDEN_SIZE), 1.0, 6.0, ((0, 512),)),
    }


slot_group = 16


def tile_sum(blocks, index_in, index_out, live_count, sources, outputs, transposed):
    groups = blocks.shape[0] // slot_group
    targets = jnp.arange(outputs, dtype=jnp.int32)

    def advance(totals, block_index):
        offset = block_index * slot_group
        tiles_now = lax.dynamic_slice_in_dim(blocks, offset, slot_group, 0).astype(jnp.float32)
        inputs_now = lax.dynamic_slice_in_dim(index_in, offset, slot_group, 0)
        outputs_now = lax.dynamic_slice_in_dim(index_out, offset, slot_group, 0)
        live = (offset + jnp.arange(slot_group, dtype=jnp.int32)) < live_count
        gathered = jnp.take(sources, inputs_now, axis=0).astype(jnp.float32)
        if transposed:
            products = jnp.einsum("bji,bjh->bih", tiles_now, gathered, precision=lax.Precision.HIGHEST)
        else:
            products = jnp.einsum("bij,bjh->bih", tiles_now, gathered, precision=lax.Precision.HIGHEST)
        selector = ((outputs_now[:, None] == targets[None, :]) & live[:, None]).astype(jnp.float32)
        added = jnp.einsum("bn,bih->nih", selector, products, precision=lax.Precision.HIGHEST)
        return totals + added, None

    start_value = jnp.zeros((outputs, blocks.shape[1], sources.shape[2]), jnp.float32)
    totals, unused = lax.scan(advance, start_value, jnp.arange(groups, dtype=jnp.int32))
    return totals


def rounded(values):
    return lax.optimization_barrier(values.astype(jnp.bfloat16)).astype(jnp.float32)


def reference(features, weight, edge_tiles, tile_row, tile_col, tile_count, labels, cotangent):
    column_blocks = features.reshape(N_ROW, N_COL, NODE_DEV, F_IN).transpose(1, 0, 2, 3)
    column_blocks = column_blocks.reshape(N_COL, CB, TILE, F_IN)

    def forward_row(row_index):
        def over_cols(total, col_index):
            part = tile_sum(edge_tiles[row_index, col_index], tile_col[row_index, col_index],
                            tile_row[row_index, col_index], tile_count[row_index, col_index],
                            column_blocks[col_index], RB, False)
            return total + rounded(part), None

        total, unused = lax.scan(over_cols, jnp.zeros((RB, TILE, F_IN), jnp.float32),
                                 jnp.arange(N_COL, dtype=jnp.int32))
        return total

    aggregate = lax.map(forward_row, jnp.arange(N_ROW, dtype=jnp.int32)).reshape(NODES, F_IN)
    aggregate = aggregate.astype(jnp.bfloat16)
    preact = jnp.dot(aggregate, weight, preferred_element_type=jnp.float32)
    activation = jax.nn.silu(preact).astype(jnp.bfloat16)
    sigmoid_v = jax.nn.sigmoid(preact)
    labelled = (labels >= 0).astype(jnp.float32)[:, None]
    grad_pre = cotangent.astype(jnp.float32) * labelled * sigmoid_v * (1.0 + preact * (1.0 - sigmoid_v))
    grad_pre = grad_pre.astype(jnp.bfloat16)
    grad_proj = jnp.dot(grad_pre, weight.T, preferred_element_type=jnp.float32).astype(jnp.bfloat16)
    row_blocks = grad_proj.reshape(N_ROW, RB, TILE, F_IN)

    def backward_col(col_index):
        def over_rows(total, row_index):
            part = tile_sum(edge_tiles[row_index, col_index], tile_row[row_index, col_index],
                            tile_col[row_index, col_index], tile_count[row_index, col_index],
                            row_blocks[row_index], CB, True)
            return total + rounded(part), None

        total, unused = lax.scan(over_rows, jnp.zeros((CB, TILE, F_IN), jnp.float32),
                                 jnp.arange(N_ROW, dtype=jnp.int32))
        return total

    summed = lax.map(backward_col, jnp.arange(N_COL, dtype=jnp.int32))
    summed = summed.reshape(N_COL, N_ROW, NODE_DEV, F_IN).transpose(1, 0, 2, 3)
    grad_features = summed.reshape(NODES, F_IN).astype(jnp.bfloat16)
    grad_weight = jnp.dot(aggregate.T, grad_pre, preferred_element_type=jnp.float32) * (float(NODES) ** -0.5)
    return activation, grad_features, grad_weight
```

```python
import jax
import jax.numpy as jnp
from jax import lax
from jax.experimental import pallas as pl
from jax.experimental.pallas import tpu as pltpu
from jax.sharding import PartitionSpec as P

MESH = pl.DeviceIdType.MESH
NX, NZ, NY = 4, 8, 8
T = 128
WIDE = 256
RING8 = (4, 3, 5, 2, 6, 1, 7)
RING4 = (2, 1, 3)
UNROLL = 8
BF, F32, I32 = jnp.bfloat16, jnp.float32, jnp.int32


def iota(shape, dim):
    return lax.broadcasted_iota(I32, shape, dim)


def mm(a, b):
    return jnp.dot(a, b, preferred_element_type=F32)


def mm_t(a, b):
    return lax.dot_general(a, b, (((1,), (1,)), ((), ())), preferred_element_type=F32)


def one_hot(mask):
    return jnp.where(mask, 1.0, 0.0).astype(BF)


def make_plan(keys, others, live, empty, out):
    groups = one_hot((iota((T, WIDE), 0) == keys) & live)
    before = one_hot(iota((WIDE, WIDE), 0) < iota((WIDE, WIDE), 1))
    rank = mm(groups, before)
    count = mm(groups, jnp.ones((WIDE, T), BF))
    padded = 2.0 * jnp.floor((count + 1.0) * 0.5)
    lower = one_hot(iota((T, T), 1) < iota((T, T), 0))
    start = mm(lower, padded.astype(BF))
    hot = groups.astype(F32)
    rank_here = jnp.sum(hot * rank, axis=0, keepdims=True)
    place = rank_here + jnp.sum(hot * start[:, :1], axis=0, keepdims=True)
    chosen = one_hot((iota((WIDE, WIDE), 0) == place.astype(I32)) & live)
    which = iota((8, WIDE), 0)
    slot = iota((8, WIDE), 1).astype(F32)
    rows = jnp.where(which == 0, slot, jnp.where(which == 1, others.astype(F32), jnp.where(
        which == 2, jnp.where(rank_here == 0.0, 1.0, 0.0), 1.0)))
    sorted_rows = mm_t(rows.astype(BF), chosen)
    count_row = mm_t(jnp.ones((8, WIDE), BF), groups)
    padded_row = 2.0 * jnp.floor((count_row + 1.0) * 0.5)
    upper = one_hot(iota((T, T), 0) < iota((T, T), 1))
    end_row = mm(padded_row.astype(BF), upper) + padded_row
    last_row = jnp.maximum(end_row * 0.5 - 1.0, 0.0)
    valid = sorted_rows[3:4] > 0.5
    out[0:1, :] = sorted_rows[0:1].astype(I32)
    out[1:2, :] = jnp.where(valid, sorted_rows[1:2], float(empty)).astype(I32)
    out[2:3, :] = (1.0 - sorted_rows[2:3]).astype(I32)
    out[3:4, 0:T] = last_row[0:1].astype(I32)
    out[4:5, 0:T] = jnp.where(count_row[0:1] > 0.5, 1.0, 0.0).astype(I32)


def kernel(features, weight, tiles, tile_row, tile_col, tile_count, labels, cotangent,
           act_out, gf_out, gw_out,
           tile_buf, xbuf, gbuf, pref, pblk, cr, ystage, yr, bblk, xr, zstage, zr, wbuf, cbuf, slots,
           plan_v, plan_f, plan_b, wt, w0r, wh, w1r, w2b, w3b, gw, act_v, gf_v,
           loc, ag_s, ag_r, c_s, c_r, y_s, y_r, g_s, g_r, x_s, x_r, z_s, z_r,
           w_s, w0_r, w1_r, w2_r, w3_r, w4_r, w5_r):
    r, c = lax.axis_index("row"), lax.axis_index("col")
    x, z, y, k = r // NZ, r % NZ, c // 2, c % 2
    other = 1 - k

    def at_x(d):
        return (((x + d) % NX) * NZ + z, c)

    def at_z(d):
        return (x * NZ + (z + d) % NZ, c)

    def at_y(d):
        return (r, ((y + d) % NY) * 2 + k)

    sibling = (r, y * 2 + other)
    sends = []

    def push(src, dst, ssem, rsem, device):
        copy = pltpu.make_async_remote_copy(src_ref=src, dst_ref=dst, send_sem=ssem, recv_sem=rsem,
                                            device_id=device, device_id_type=MESH)
        copy.start()
        sends.append(copy)

    def arrived(dst, sem):
        pltpu.make_async_remote_copy(src_ref=dst, dst_ref=dst, send_sem=sem, recv_sem=sem,
                                     device_id=sibling, device_id_type=MESH).wait_recv()

    barrier = pltpu.get_barrier_semaphore()
    partners = [at_z(d) for d in RING8] + [at_x(d) for d in RING4] + [at_y(d) for d in RING8] + [sibling]
    for device in partners:
        pl.semaphore_signal(barrier, inc=1, device_id=device, device_id_type=MESH)
    own = pltpu.make_async_copy(features, xbuf.at[0], loc.at[0])
    own.start()
    part = tiles.shape[0] // 4
    edge = [pltpu.make_async_copy(tiles.at[pl.ds(i * part, part)], tile_buf.at[pl.ds(i * part, part)], loc.at[1 + i])
            for i in range(4)]
    wcopy = pltpu.make_async_copy(weight, wbuf, loc.at[5])
    ccopy = pltpu.make_async_copy(cotangent, cbuf, loc.at[6])
    own.wait()
    pl.semaphore_wait(barrier, len(partners))

    for dz in RING8:
        push(xbuf.at[0], xbuf.at[dz], ag_s.at[dz], ag_r.at[dz], at_z(dz))
    for dx in RING4:
        push(xbuf.at[0], xbuf.at[dx * NZ], ag_s.at[dx * NZ], ag_r.at[dx * NZ], at_x(dx))
    for copy in edge + [wcopy, ccopy]:
        copy.start()

    slots[...] = jnp.zeros_like(slots)
    plan_v[...] = jnp.zeros_like(plan_v)
    slots[0:1, 0:tile_row.shape[1]] = tile_row[...]
    slots[1:2, 0:tile_row.shape[1]] = tile_col[...]
    rows_here, cols_here = slots[0:1, :], slots[1:2, :]
    live = iota((1, WIDE), 1) < tile_count[0, 0]
    xbuf[NX * NZ] = jnp.zeros((T, T), BF)
    gbuf[NY * 2] = jnp.zeros((T, T), BF)
    to_row = ((rows_here // 2 - y + NY) % NY) * 2 + (rows_here + k) % 2
    from_row = ((y - rows_here // 2 + NY) % NY) * 2 + (rows_here + k) % 2
    to_col = ((cols_here // NZ - x + NX) % NX) * NZ + (cols_here - z + NZ) % NZ
    from_col = ((x - cols_here // NZ + NX) % NX) * NZ + (z - cols_here + 4 * NZ) % NZ
    make_plan(to_row, from_col, live, NX * NZ, plan_v.at[0])
    make_plan(to_col, from_row, live, NY * 2, plan_v.at[1])
    fcopy = pltpu.make_async_copy(plan_v.at[0], plan_f, loc.at[7])
    bcopy = pltpu.make_async_copy(plan_v.at[1], plan_b, loc.at[8])
    fcopy.start()
    bcopy.start()

    for dz in (1, 7, 2, 6, 3, 5, 4):
        arrived(xbuf.at[dz], ag_r.at[dz])
        for dx in RING4:
            s = dx * NZ + dz
            push(xbuf.at[dz], xbuf.at[s], ag_s.at[s], ag_r.at[s], at_x(dx))
    for copy in edge + [wcopy, ccopy, fcopy, bcopy]:
        copy.wait()
    for dz in (0, 1, 7, 2, 6, 3, 5, 4):
        for dx in (1, 3, 2):
            arrived(xbuf.at[dx * NZ + dz], ag_r.at[dx * NZ + dz])

    def within(index, size):
        return jnp.minimum(jnp.maximum(index, 0), size - 1)

    def run(plan, pairs, blocks, product):
        def body(step, total):
            for u in range(UNROLL):
                pair = step * UNROLL + u
                first, second = 2 * pair, 2 * pair + 1
                value = product(
                    within(plan[0, first], tile_buf.shape[0]), within(plan[0, second], tile_buf.shape[0]),
                    within(plan[1, first], blocks), within(plan[1, second], blocks))
                total = jnp.where(plan[2, first] > 0, total, 0.0) + value
                pref[pair] = total
            return total

        lax.fori_loop(0, pairs // UNROLL, body, jnp.zeros((T, T), F32))

    def result(plan, group):
        return jnp.where(plan[4, group] > 0, pref[within(plan[3, group], pref.shape[0])], 0.0).astype(BF)

    def forward(s0, s1, b0, b1):
        return mm(jnp.concatenate([tile_buf[s0], tile_buf[s1]], axis=1),
                  jnp.concatenate([xbuf[b0], xbuf[b1]], axis=0))

    def backward(s0, s1, b0, b1):
        return mm(jnp.concatenate([gbuf[b0], gbuf[b1]], axis=1),
                  jnp.concatenate([tile_buf[s0], tile_buf[s1]], axis=0))

    slots_all = tiles.shape[0]
    run(plan_f, (slots_all + NY * 2) // 2, xbuf.shape[0], forward)

    for ey in RING8 + (0,):
        pblk[ey * 2 + 1] = result(plan_f, ey * 2 + 1)
        push(pblk.at[ey * 2 + 1], cr.at[ey], c_s.at[ey], c_r.at[ey], sibling)
    for ey in RING8 + (0,):
        pblk[ey * 2] = result(plan_f, ey * 2)
    for ey in RING8:
        arrived(cr.at[ey], c_r.at[ey])
        ystage[ey] = (pblk[ey * 2].astype(F32) + cr[ey].astype(F32)).astype(BF)
        push(ystage.at[ey], yr.at[ey], y_s.at[ey], y_r.at[ey], at_y(ey))
    arrived(cr.at[0], c_r.at[0])
    total = pblk[0].astype(F32) + cr[0].astype(F32)
    diagonal = jnp.where(iota((T, T), 0) == iota((T, T), 1), jnp.where(labels[...] >= 0, 1.0, 0.0), 0.0).astype(BF)
    masked = cbuf[...].astype(F32) * mm(diagonal, jnp.ones((T, WIDE), BF))
    for ey in (1, 7, 2, 6, 3, 5, 4):
        arrived(yr.at[ey], y_r.at[ey])
        total = total + yr[ey].astype(F32)
    aggregate = total.astype(BF)
    preact = mm(aggregate, wbuf[...])
    sigmoid_v = jax.nn.sigmoid(preact)
    grad_pre = (masked * sigmoid_v * (1.0 + preact * (1.0 - sigmoid_v))).astype(BF)
    gbuf[0] = mm_t(wbuf[...], grad_pre).astype(BF)

    for dy in RING8:
        push(gbuf.at[0], gbuf.at[dy * 2], g_s.at[dy * 2], g_r.at[dy * 2], at_y(dy))
    push(gbuf.at[0], gbuf.at[1], g_s.at[1], g_r.at[1], sibling)
    act_v[...] = (preact * sigmoid_v).astype(BF)
    acopy = pltpu.make_async_copy(act_v, act_out, loc.at[9])
    acopy.start()
    wt[...] = lax.dot_general(aggregate, grad_pre, (((0,), (0,)), ((), ())), preferred_element_type=F32)
    half = T // 2
    mine = pl.ds(pl.multiple_of(k * half, half), half)
    theirs = pl.ds(pl.multiple_of(other * half, half), half)
    push(wt.at[theirs], w0r, w_s.at[0], w0_r, sibling)
    arrived(w0r, w0_r)
    wh[...] = wt[mine, :] + w0r[...]
    piece = half // NY

    def rows_of(d):
        return pl.ds(pl.multiple_of(((y + d) % NY) * piece, piece), piece)

    for ey in RING8:
        push(wh.at[rows_of(ey)], w1r.at[ey], w_s.at[ey], w1_r.at[ey], at_y(ey))
    for dy in (1, 7, 2, 6, 3, 5, 4):
        arrived(gbuf.at[dy * 2], g_r.at[dy * 2])
        push(gbuf.at[dy * 2], gbuf.at[dy * 2 + 1], g_s.at[dy * 2 + 1], g_r.at[dy * 2 + 1], sibling)
    for dy in (0, 1, 7, 2, 6, 3, 5, 4):
        arrived(gbuf.at[dy * 2 + 1], g_r.at[dy * 2 + 1])
    term = wh[rows_of(0), :]
    for ey in RING8:
        arrived(w1r.at[ey], w1_r.at[ey])
        term = term + w1r[ey]
    w2b[z] = term
    for dz in RING8:
        push(w2b.at[z], w2b.at[z], w_s.at[8 + dz], w2_r.at[dz], at_z(dz))

    run(plan_b, (slots_all + NX * NZ) // 2, gbuf.shape[0], backward)

    for ez in RING8 + (0,):
        for ex in RING4:
            g = ex * NZ + ez
            bblk[g] = result(plan_b, g)
            push(bblk.at[g], xr.at[g], x_s.at[g], x_r.at[g], at_x(ex))
    for ez in range(NZ):
        bblk[ez] = result(plan_b, ez)
    for dz in RING8:
        arrived(w2b.at[(z + NZ - dz) % NZ], w2_r.at[dz])
    term = w2b[0]
    for i in range(1, NZ):
        term = term + w2b[i]
    w3b[x] = term
    for dx in RING4:
        push(w3b.at[x], w3b.at[x], w_s.at[16 + dx], w3_r.at[dx], at_x(dx))

    def x_total(ez):
        total = bblk[ez].astype(F32)
        for ex in (1, 3, 2):
            g = ex * NZ + ez
            arrived(xr.at[g], x_r.at[g])
            total = total + xr[g].astype(F32)
        return total

    for ez in RING8:
        zstage[ez] = x_total(ez).astype(BF)
        push(zstage.at[ez], zr.at[ez], z_s.at[ez], z_r.at[ez], at_z(ez))
    total = x_total(0)
    for dx in RING4:
        arrived(w3b.at[(x + NX - dx) % NX], w3_r.at[dx])
    term = w3b[0]
    for i in range(1, NX):
        term = term + w3b[i]

    def gw_rows(d):
        return pl.ds(pl.multiple_of(k * half + ((y + NY + d) % NY) * piece, piece), piece)

    gw[gw_rows(0), :] = term * (float(T * NX * NZ * NY * 2) ** -0.5)
    for dy in RING8:
        push(gw.at[gw_rows(0)], gw.at[gw_rows(0)], w_s.at[20 + dy], w4_r.at[dy], at_y(dy))
    for dy in RING8:
        arrived(gw.at[gw_rows(-dy)], w4_r.at[dy])
    push(gw.at[mine], gw.at[mine], w_s.at[28], w5_r, sibling)
    for ez in (1, 7, 2, 6, 3, 5, 4):
        arrived(zr.at[ez], z_r.at[ez])
        total = total + zr[ez].astype(F32)
    gf_v[...] = jnp.transpose(total).astype(BF)
    ocopy = pltpu.make_async_copy(gf_v, gf_out, loc.at[10])
    ocopy.start()
    arrived(gw.at[theirs], w5_r)
    gcopy = pltpu.make_async_copy(gw, gw_out, loc.at[11])
    gcopy.start()
    for copy in sends:
        copy.wait_send()
    acopy.wait()
    ocopy.wait()
    gcopy.wait()


def shards(features, weight, edge_tiles, tile_row, tile_col, tile_count, labels, cotangent):
    count = edge_tiles.shape[2]
    nodes, width = features.shape
    hidden = weight.shape[1]
    pairs = (count + NX * NZ) // 2
    dma = pltpu.SemaphoreType.DMA
    anywhere = pl.BlockSpec(memory_space=pl.ANY)
    vmem = pl.BlockSpec(memory_space=pltpu.VMEM)
    smem = pl.BlockSpec(memory_space=pltpu.SMEM)
    V = pltpu.VMEM
    return pl.pallas_call(
        kernel,
        out_shape=(
            jax.ShapeDtypeStruct((nodes, hidden), BF),
            jax.ShapeDtypeStruct((nodes, width), BF),
            jax.ShapeDtypeStruct((width, hidden), F32),
        ),
        in_specs=[anywhere, anywhere, anywhere, vmem, vmem, smem, vmem, anywhere],
        out_specs=(anywhere, anywhere, anywhere),
        scratch_shapes=[
            V((count, T, T), BF),
            V((NX * NZ + 1, T, T), BF),
            V((NY * 2 + 1, T, T), BF),
            V((pairs, T, T), F32),
            V((NY * 2, T, T), BF),
            V((NY, T, T), BF),
            V((NY, T, T), BF),
            V((NY, T, T), BF),
            V((NX * NZ, T, T), BF),
            V((NX * NZ, T, T), BF),
            V((NZ, T, T), BF),
            V((NZ, T, T), BF),
            V((width, hidden), BF),
            V((nodes, hidden), BF),
            V((8, WIDE), I32),
            V((2, 8, WIDE), I32),
            pltpu.SMEM((8, WIDE), I32),
            pltpu.SMEM((8, WIDE), I32),
            V((width, hidden), F32),
            V((width // 2, hidden), F32),
            V((width // 2, hidden), F32),
            V((NY, width // 2 // NY, hidden), F32),
            V((NZ, width // 2 // NY, hidden), F32),
            V((NX, width // 2 // NY, hidden), F32),
            V((width, hidden), F32),
            V((nodes, hidden), BF),
            V((nodes, width), BF),
            dma((12,)),
            dma((NX * NZ,)), dma((NX * NZ,)),
            dma((NY,)), dma((NY,)),
            dma((NY,)), dma((NY,)),
            dma((NY * 2,)), dma((NY * 2,)),
            dma((NX * NZ,)), dma((NX * NZ,)),
            dma((NZ,)), dma((NZ,)),
            dma((30,)),
            dma, dma((NY,)), dma((NZ,)), dma((NX,)), dma((NY,)), dma,
        ],
        compiler_params=pltpu.CompilerParams(
            collective_id=0, has_side_effects=True, vmem_limit_bytes=48 * 1024 * 1024
        ),
    )(features, weight, edge_tiles.reshape(count, T, T), tile_row.reshape(1, count), tile_col.reshape(1, count),
      tile_count, labels.reshape(1, nodes), cotangent)


def solution(mesh):
    return jax.shard_map(
        shards,
        mesh=mesh,
        in_specs=(
            P(("row", "col"), None),
            P(),
            P("row", "col", None, None, None),
            P("row", "col", None),
            P("row", "col", None),
            P("row", "col"),
            P(("row", "col")),
            P(("row", "col"), None),
        ),
        out_specs=(P(("row", "col"), None), P(("row", "col"), None), P()),
        check_vma=False,
    )
```

```python
import jax
import jax.numpy as jnp
from jax import lax
from jax.experimental import pallas as pl
from jax.experimental.pallas import tpu as pltpu
from jax.sharding import PartitionSpec as P

MESH = pl.DeviceIdType.MESH
NX, NZ, NY = 4, 8, 8
T = 128
WIDE = 256
RING8 = (4, 3, 5, 2, 6, 1, 7)
RING4 = (2, 1, 3)
FORWARD_STEP, BACKWARD_STEP = 20, 22
HALF = 64
BF, F32, I32 = jnp.bfloat16, jnp.float32, jnp.int32


def iota(shape, dim):
    return lax.broadcasted_iota(I32, shape, dim)


def mm(a, b):
    return jnp.dot(a, b, preferred_element_type=F32)


def mm_t(a, b):
    return lax.dot_general(a, b, (((1,), (1,)), ((), ())), preferred_element_type=F32)


def one_hot(mask):
    return jnp.where(mask, 1.0, 0.0).astype(BF)


def make_plan(keys, others, live, empty, out):
    groups = one_hot((iota((T, WIDE), 0) == keys) & live)
    before = one_hot(iota((WIDE, WIDE), 0) < iota((WIDE, WIDE), 1))
    rank = mm(groups, before)
    count = mm(groups, jnp.ones((WIDE, T), BF))
    padded = 2.0 * jnp.floor((count + 1.0) * 0.5)
    lower = one_hot(iota((T, T), 1) < iota((T, T), 0))
    start = mm(lower, padded.astype(BF))
    hot = groups.astype(F32)
    rank_here = jnp.sum(hot * rank, axis=0, keepdims=True)
    place = rank_here + jnp.sum(hot * start[:, :1], axis=0, keepdims=True)
    chosen = one_hot((iota((WIDE, WIDE), 0) == place.astype(I32)) & live)
    which = iota((8, WIDE), 0)
    slot = iota((8, WIDE), 1).astype(F32)
    rows = jnp.where(which == 0, slot, jnp.where(which == 1, others.astype(F32), jnp.where(
        which == 2, jnp.where(rank_here == 0.0, 1.0, 0.0), 1.0)))
    sorted_rows = mm_t(rows.astype(BF), chosen)
    count_row = mm_t(jnp.ones((8, WIDE), BF), groups)
    padded_row = 2.0 * jnp.floor((count_row + 1.0) * 0.5)
    upper = one_hot(iota((T, T), 0) < iota((T, T), 1))
    end_row = mm(padded_row.astype(BF), upper) + padded_row
    last_row = jnp.maximum(end_row * 0.5 - 1.0, 0.0)
    valid = sorted_rows[3:4] > 0.5
    out[0:1, :] = sorted_rows[0:1].astype(I32)
    out[1:2, :] = jnp.where(valid, sorted_rows[1:2], float(empty)).astype(I32)
    out[2:3, :] = (1.0 - sorted_rows[2:3]).astype(I32)
    out[3:4, 0:T] = last_row[0:1].astype(I32)
    out[4:5, 0:T] = jnp.where(count_row[0:1] > 0.5, 1.0, 0.0).astype(I32)


def kernel(features, weight, tiles, tile_row, tile_col, labels, cotangent, tile_count,
           act_out, gf_out, gw_out,
           tile_buf, xbuf, gbuf_a, gbuf_b, pref, pref2, pblk, cr, ystage, yr, bblk, xr, zstage, zr, wbuf, cbuf, slots,
           plan_v, plan_f, plan_b, wt, w0r, wh, w1r, w2b, w3b, rows_v, cols_v, labels_v,
           loc, ag_s, ag_r, c_s, c_r, y_s, y_r, g_s, g_r, x_s, x_r, z_s, z_r,
           w_s, w0_r, w1_r, w2_r, w3_r, w4_r, w5_r):
    r, c = lax.axis_index("row"), lax.axis_index("col")
    gbuf = (gbuf_a, gbuf_b)
    x, z, y, k = r // NZ, r % NZ, c // 2, c % 2
    other = 1 - k

    def at_x(d):
        return (((x + d) % NX) * NZ + z, c)

    def at_z(d):
        return (x * NZ + (z + d) % NZ, c)

    def at_y(d):
        return (r, ((y + d) % NY) * 2 + k)

    sibling = (r, y * 2 + other)
    sends = []

    def push(src, dst, ssem, rsem, device):
        copy = pltpu.make_async_remote_copy(src_ref=src, dst_ref=dst, send_sem=ssem, recv_sem=rsem,
                                            device_id=device, device_id_type=MESH)
        copy.start()
        sends.append(copy)

    def arrived(dst, sem):
        pltpu.make_async_remote_copy(src_ref=dst, dst_ref=dst, send_sem=sem, recv_sem=sem,
                                     device_id=sibling, device_id_type=MESH).wait_recv()

    own = pltpu.make_async_copy(features, xbuf.at[0], loc.at[0])
    own.start()
    barrier = pltpu.get_barrier_semaphore()
    partners = [at_z(d) for d in RING8] + [at_x(d) for d in RING4] + [at_y(d) for d in RING8] + [sibling]
    for device in partners:
        pl.semaphore_signal(barrier, inc=1, device_id=device, device_id_type=MESH)
    part = tiles.shape[0] // 4
    edge = [pltpu.make_async_copy(tiles.at[pl.ds(i * part, part)], tile_buf.at[pl.ds(i * part, part)], loc.at[1 + i])
            for i in range(4)]
    wcopy = pltpu.make_async_copy(weight, wbuf, loc.at[5])
    ccopy = pltpu.make_async_copy(cotangent, cbuf, loc.at[6])
    small = [pltpu.make_async_copy(a, b, loc.at[9 + i]) for i, (a, b) in enumerate(
        ((tile_row, rows_v), (tile_col, cols_v), (labels, labels_v)))]
    for copy in small + edge + [wcopy, ccopy]:
        copy.start()
    own.wait()
    pl.semaphore_wait(barrier, len(partners))

    for dz in RING8:
        push(xbuf.at[0], xbuf.at[dz], ag_s.at[dz], ag_r.at[dz], at_z(dz))
    for dx in RING4:
        push(xbuf.at[0], xbuf.at[dx * NZ], ag_s.at[dx * NZ], ag_r.at[dx * NZ], at_x(dx))
    for copy in small:
        copy.wait()
    slots[...] = jnp.zeros_like(slots)
    plan_v[...] = jnp.zeros_like(plan_v)
    slots[0:1, 0:tile_row.shape[1]] = rows_v[...]
    slots[1:2, 0:tile_row.shape[1]] = cols_v[...]
    rows_here, cols_here = slots[0:1, :], slots[1:2, :]
    live = iota((1, WIDE), 1) < tile_count[0, 0]
    xbuf[NX * NZ] = jnp.zeros((T, T), BF)
    for h in range(2):
        gbuf[h][NY * 2] = jnp.zeros((HALF, T), BF)
    to_row = ((rows_here // 2 - y + NY) % NY) * 2 + (rows_here + k) % 2
    from_row = ((y - rows_here // 2 + NY) % NY) * 2 + (rows_here + k) % 2
    to_col = ((cols_here // NZ - x + NX) % NX) * NZ + (cols_here - z + NZ) % NZ
    from_col = ((x - cols_here // NZ + NX) % NX) * NZ + (z - cols_here + 4 * NZ) % NZ
    make_plan(to_row, from_col, live, NX * NZ, plan_v.at[0])
    make_plan(to_col, from_row, live, NY * 2, plan_v.at[1])
    fcopy = pltpu.make_async_copy(plan_v.at[0], plan_f, loc.at[7])
    bcopy = pltpu.make_async_copy(plan_v.at[1], plan_b, loc.at[8])
    fcopy.start()
    bcopy.start()

    for dz in (1, 7, 2, 6, 3, 5, 4):
        arrived(xbuf.at[dz], ag_r.at[dz])
        for dx in RING4:
            s = dx * NZ + dz
            push(xbuf.at[dz], xbuf.at[s], ag_s.at[s], ag_r.at[s], at_x(dx))
    for copy in edge + [wcopy, ccopy, fcopy, bcopy]:
        copy.wait()
    for dz in (0, 1, 7, 2, 6, 3, 5, 4):
        for dx in (1, 3, 2):
            arrived(xbuf.at[dx * NZ + dz], ag_r.at[dx * NZ + dz])

    def within(index, size):
        return jnp.minimum(jnp.maximum(index, 0), size - 1)

    def run(plan, pairs, unroll, blocks, sums, product):
        def body(step, total):
            for u in range(unroll):
                pair = step * unroll + u
                first, second = 2 * pair, 2 * pair + 1
                value = product(
                    within(plan[0, first], tile_buf.shape[0]), within(plan[0, second], tile_buf.shape[0]),
                    within(plan[1, first], blocks), within(plan[1, second], blocks))
                total = jnp.where(plan[2, first] > 0, total, 0.0) + value
                sums[pair] = total
            return total

        lax.fori_loop(0, pairs // unroll, body, jnp.zeros(sums.shape[1:], F32))

    def result(plan, group, sums):
        return jnp.where(plan[4, group] > 0, sums[within(plan[3, group], sums.shape[0])], 0.0).astype(BF)

    def forward(s0, s1, b0, b1):
        return mm(jnp.concatenate([tile_buf[s0], tile_buf[s1]], axis=1),
                  jnp.concatenate([xbuf[b0], xbuf[b1]], axis=0))

    def backward(h):
        def product(s0, s1, b0, b1):
            return mm(jnp.concatenate([gbuf[h][b0], gbuf[h][b1]], axis=1),
                      jnp.concatenate([tile_buf[s0], tile_buf[s1]], axis=0))
        return product

    slots_all = tiles.shape[0]
    run(plan_f, (slots_all + NY * 2) // 2, FORWARD_STEP, xbuf.shape[0], pref, forward)

    for ey in RING8 + (0,):
        pblk[ey * 2 + 1] = result(plan_f, ey * 2 + 1, pref)
        push(pblk.at[ey * 2 + 1], cr.at[ey], c_s.at[ey], c_r.at[ey], sibling)
    for ey in RING8 + (0,):
        pblk[ey * 2] = result(plan_f, ey * 2, pref)
    for ey in RING8:
        arrived(cr.at[ey], c_r.at[ey])
        ystage[ey] = (pblk[ey * 2].astype(F32) + cr[ey].astype(F32)).astype(BF)
        push(ystage.at[ey], yr.at[ey], y_s.at[ey], y_r.at[ey], at_y(ey))
    arrived(cr.at[0], c_r.at[0])
    total = pblk[0].astype(F32) + cr[0].astype(F32)
    diagonal = jnp.where(iota((T, T), 0) == iota((T, T), 1), jnp.where(labels_v[...] >= 0, 1.0, 0.0), 0.0).astype(BF)
    masked = cbuf[...].astype(F32) * mm(diagonal, jnp.ones((T, WIDE), BF))
    for ey in (1, 7, 2, 6, 3, 5, 4):
        arrived(yr.at[ey], y_r.at[ey])
        total = total + yr[ey].astype(F32)
    aggregate = total.astype(BF)
    preact = mm(aggregate, wbuf[...])
    sigmoid_v = jax.nn.sigmoid(preact)
    grad_pre = (masked * sigmoid_v * (1.0 + preact * (1.0 - sigmoid_v))).astype(BF)
    projected = mm_t(wbuf[...], grad_pre).astype(BF)
    gbuf[0][0] = projected[:HALF]
    gbuf[1][0] = projected[HALF:]

    for h in range(2):
        for dy in RING8:
            push(gbuf[h].at[0], gbuf[h].at[dy * 2], g_s.at[h, dy * 2], g_r.at[h, dy * 2], at_y(dy))
        push(gbuf[h].at[0], gbuf[h].at[1], g_s.at[h, 1], g_r.at[h, 1], sibling)
    act_out[...] = (preact * sigmoid_v).astype(BF)
    wt[...] = lax.dot_general(aggregate, grad_pre, (((0,), (0,)), ((), ())), preferred_element_type=F32)
    half = T // 2
    mine = pl.ds(pl.multiple_of(k * half, half), half)
    theirs = pl.ds(pl.multiple_of(other * half, half), half)
    push(wt.at[theirs], w0r, w_s.at[0], w0_r, sibling)
    arrived(w0r, w0_r)
    wh[...] = wt[mine, :] + w0r[...]
    piece = half // NY

    def rows_of(d):
        return pl.ds(pl.multiple_of(((y + d) % NY) * piece, piece), piece)

    for ey in RING8:
        push(wh.at[rows_of(ey)], w1r.at[ey], w_s.at[ey], w1_r.at[ey], at_y(ey))
    def hand_on(h):
        for dy in (1, 7, 2, 6, 3, 5, 4):
            arrived(gbuf[h].at[dy * 2], g_r.at[h, dy * 2])
            push(gbuf[h].at[dy * 2], gbuf[h].at[dy * 2 + 1], g_s.at[h, dy * 2 + 1], g_r.at[h, dy * 2 + 1], sibling)

    def transposed_sums(h):
        for dy in (0, 1, 7, 2, 6, 3, 5, 4):
            arrived(gbuf[h].at[dy * 2 + 1], g_r.at[h, dy * 2 + 1])
        run(plan_b, (slots_all + NX * NZ) // 2, BACKWARD_STEP, gbuf[h].shape[0], pref2.at[h], backward(h))

    def send_x(h):
        for ez in RING8 + (0,):
            for ex in RING4:
                g = ex * NZ + ez
                bblk[h, g] = result(plan_b, g, pref2.at[h])
                push(bblk.at[h, g], xr.at[h, g], x_s.at[h, g], x_r.at[h, g], at_x(ex))
        for ez in range(NZ):
            bblk[h, ez] = result(plan_b, ez, pref2.at[h])

    hand_on(0)
    transposed_sums(0)
    hand_on(1)
    term = wh[rows_of(0), :]
    for ey in RING8:
        arrived(w1r.at[ey], w1_r.at[ey])
        term = term + w1r[ey]
    w2b[x] = term
    for dx in RING4:
        push(w2b.at[x], w2b.at[x], w_s.at[8 + dx], w2_r.at[dx], at_x(dx))

    send_x(0)
    transposed_sums(1)
    send_x(1)
    for dx in RING4:
        arrived(w2b.at[(x + NX - dx) % NX], w2_r.at[dx])
    term = w2b[0]
    for i in range(1, NX):
        term = term + w2b[i]
    w3b[z] = term
    for dz in RING8:
        push(w3b.at[z], w3b.at[z], w_s.at[12 + dz], w3_r.at[dz], at_z(dz))

    def x_total(h, ez):
        total = bblk[h, ez].astype(F32)
        for ex in (1, 3, 2):
            g = ex * NZ + ez
            arrived(xr.at[h, g], x_r.at[h, g])
            total = total + xr[h, g].astype(F32)
        return total

    def gw_rows(d):
        return pl.ds(pl.multiple_of(k * half + ((y + NY + d) % NY) * piece, piece), piece)

    def send_z(h):
        for ez in RING8:
            zstage[h, ez] = x_total(h, ez).astype(BF)
            push(zstage.at[h, ez], zr.at[h, ez], z_s.at[h, ez], z_r.at[h, ez], at_z(ez))

    send_z(0)
    for dz in RING8:
        arrived(w3b.at[(z + NZ - dz) % NZ], w3_r.at[dz])
    term = w3b[0]
    for i in range(1, NZ):
        term = term + w3b[i]
    gw_out[gw_rows(0), :] = term * (float(T * NX * NZ * NY * 2) ** -0.5)
    for dy in RING8:
        push(gw_out.at[gw_rows(0)], gw_out.at[gw_rows(0)], w_s.at[20 + dy], w4_r.at[dy], at_y(dy))
    total_a = x_total(0, 0)
    send_z(1)
    total_b = x_total(1, 0)
    for dy in RING8:
        arrived(gw_out.at[gw_rows(-dy)], w4_r.at[dy])
    push(gw_out.at[mine], gw_out.at[mine], w_s.at[28], w5_r, sibling)
    for ez in (1, 7, 2, 6, 3, 5, 4):
        arrived(zr.at[0, ez], z_r.at[0, ez])
        total_a = total_a + zr[0, ez].astype(F32)
    for ez in (1, 7, 2, 6, 3, 5, 4):
        arrived(zr.at[1, ez], z_r.at[1, ez])
        total_b = total_b + zr[1, ez].astype(F32)
    gf_out[...] = jnp.transpose(jnp.concatenate([total_a, total_b], axis=0)).astype(BF)
    arrived(gw_out.at[theirs], w5_r)
    for copy in sends:
        copy.wait_send()


def shards(features, weight, edge_tiles, tile_row, tile_col, tile_count, labels, cotangent):
    count = edge_tiles.shape[2]
    nodes, width = features.shape
    hidden = weight.shape[1]
    pairs = (count + NX * NZ) // 2
    dma = pltpu.SemaphoreType.DMA
    hbm = pl.BlockSpec(memory_space=pltpu.HBM)
    vmem = pl.BlockSpec(memory_space=pltpu.VMEM)
    V = pltpu.VMEM
    return pl.pallas_call(
        kernel,
        out_shape=(
            jax.ShapeDtypeStruct((nodes, hidden), BF),
            jax.ShapeDtypeStruct((nodes, width), BF),
            jax.ShapeDtypeStruct((width, hidden), F32),
        ),
        in_specs=[hbm] * 7 + [pl.BlockSpec(memory_space=pltpu.SMEM)],
        out_specs=(vmem, vmem, vmem),
        scratch_shapes=[
            V((count, T, T), BF),
            V((NX * NZ + 1, T, T), BF),
            V((NY * 2 + 1, HALF, T), BF),
            V((NY * 2 + 1, HALF, T), BF),
            V(((count + NY * 2) // 2, T, T), F32),
            V((2, pairs, HALF, T), F32),
            V((NY * 2, T, T), BF),
            V((NY, T, T), BF),
            V((NY, T, T), BF),
            V((NY, T, T), BF),
            V((2, NX * NZ, HALF, T), BF),
            V((2, NX * NZ, HALF, T), BF),
            V((2, NZ, HALF, T), BF),
            V((2, NZ, HALF, T), BF),
            V((width, hidden), BF),
            V((nodes, hidden), BF),
            V((8, WIDE), I32),
            V((2, 8, WIDE), I32),
            pltpu.SMEM((8, WIDE), I32),
            pltpu.SMEM((8, WIDE), I32),
            V((width, hidden), F32),
            V((width // 2, hidden), F32),
            V((width // 2, hidden), F32),
            V((NY, width // 2 // NY, hidden), F32),
            V((NX, width // 2 // NY, hidden), F32),
            V((NZ, width // 2 // NY, hidden), F32),
            V((1, count), I32), V((1, count), I32), V((1, nodes), I32),
            dma((13,)),
            dma((NX * NZ,)), dma((NX * NZ,)),
            dma((NY,)), dma((NY,)),
            dma((NY,)), dma((NY,)),
            dma((2, NY * 2)), dma((2, NY * 2)),
            dma((2, NX * NZ)), dma((2, NX * NZ)),
            dma((2, NZ)), dma((2, NZ)),
            dma((30,)),
            dma, dma((NY,)), dma((NX,)), dma((NZ,)), dma((NY,)), dma,
        ],
        compiler_params=pltpu.CompilerParams(
            collective_id=0, has_side_effects=True, vmem_limit_bytes=40 * 1024 * 1024
        ),
    )(*(pltpu.with_memory_space_constraint(a, pltpu.HBM) for a in (
        features, weight, edge_tiles.reshape(count, T, T), tile_row.reshape(1, count), tile_col.reshape(1, count),
        labels.reshape(1, nodes), cotangent)), tile_count)


def solution(mesh):
    return jax.shard_map(
        shards,
        mesh=mesh,
        in_specs=(
            P(("row", "col"), None),
            P(),
            P("row", "col", None, None, None),
            P("row", "col", None),
            P("row", "col", None),
            P("row", "col"),
            P(("row", "col")),
            P(("row", "col"), None),
        ),
        out_specs=(P(("row", "col"), None), P(("row", "col"), None), P()),
        check_vma=False,
    )
```

```python
import jax
import jax.numpy as jnp
from jax import lax
from jax.experimental import pallas as pl
from jax.experimental.pallas import tpu as pltpu
from jax.sharding import PartitionSpec as P

MESH = pl.DeviceIdType.MESH
NX, NZ, NY = 4, 8, 8
T = 128
WIDE = 256
RING8 = (4, 3, 5, 2, 6, 1, 7)
RING4 = (2, 1, 3)
FORWARD_STEP, BACKWARD_STEP = 20, 22
HALF = 64
BF, F32, I32 = jnp.bfloat16, jnp.float32, jnp.int32


def iota(shape, dim):
    return lax.broadcasted_iota(I32, shape, dim)


def mm(a, b):
    return jnp.dot(a, b, preferred_element_type=F32)


def mm_t(a, b):
    return lax.dot_general(a, b, (((1,), (1,)), ((), ())), preferred_element_type=F32)


def one_hot(mask):
    return jnp.where(mask, 1.0, 0.0).astype(BF)


def make_plan(keys, others, live, empty, out):
    groups = one_hot((iota((T, WIDE), 0) == keys) & live)
    before = one_hot(iota((WIDE, WIDE), 0) < iota((WIDE, WIDE), 1))
    rank = mm(groups, before)
    count = mm(groups, jnp.ones((WIDE, T), BF))
    padded = 2.0 * jnp.floor((count + 1.0) * 0.5)
    lower = one_hot(iota((T, T), 1) < iota((T, T), 0))
    start = mm(lower, padded.astype(BF))
    hot = groups.astype(F32)
    rank_here = jnp.sum(hot * rank, axis=0, keepdims=True)
    place = rank_here + jnp.sum(hot * start[:, :1], axis=0, keepdims=True)
    chosen = one_hot((iota((WIDE, WIDE), 0) == place.astype(I32)) & live)
    which = iota((8, WIDE), 0)
    slot = iota((8, WIDE), 1).astype(F32)
    rows = jnp.where(which == 0, slot, jnp.where(which == 1, others.astype(F32), jnp.where(
        which == 2, jnp.where(rank_here == 0.0, 1.0, 0.0), 1.0)))
    sorted_rows = mm_t(rows.astype(BF), chosen)
    count_row = mm_t(jnp.ones((8, WIDE), BF), groups)
    padded_row = 2.0 * jnp.floor((count_row + 1.0) * 0.5)
    upper = one_hot(iota((T, T), 0) < iota((T, T), 1))
    end_row = mm(padded_row.astype(BF), upper) + padded_row
    last_row = jnp.maximum(end_row * 0.5 - 1.0, 0.0)
    valid = sorted_rows[3:4] > 0.5
    out[0:1, :] = sorted_rows[0:1].astype(I32)
    out[1:2, :] = jnp.where(valid, sorted_rows[1:2], float(empty)).astype(I32)
    out[2:3, :] = (1.0 - sorted_rows[2:3]).astype(I32)
    out[3:4, 0:T] = last_row[0:1].astype(I32)
    out[4:5, 0:T] = jnp.where(count_row[0:1] > 0.5, 1.0, 0.0).astype(I32)


def kernel(features, weight, tiles, tile_row, tile_col, labels, cotangent, tile_count,
           act_out, gf_out, gw_out,
           tile_buf, xbuf, gbuf_a, gbuf_b, pref, pref2, pblk, cr, ystage, yr, bblk, xr, zstage, zr, wbuf, cbuf, slots,
           plan_v, plan_f, plan_b, wt, w0r, wh, w1r, w2b, w3b, rows_v, cols_v, labels_v,
           loc, ag_s, ag_r, c_s, c_r, y_s, y_r, g_s, g_r, x_s, x_r, z_s, z_r,
           w_s, w0_r, w1_r, w2_r, w3_r, w4_r, w5_r):
    r, c = lax.axis_index("row"), lax.axis_index("col")
    gbuf = (gbuf_a, gbuf_b)
    x, z, y, k = r // NZ, r % NZ, c // 2, c % 2
    other = 1 - k

    def at_x(d):
        return (((x + d) % NX) * NZ + z, c)

    def at_z(d):
        return (x * NZ + (z + d) % NZ, c)

    def at_y(d):
        return (r, ((y + d) % NY) * 2 + k)

    sibling = (r, y * 2 + other)
    sends = []

    def push(src, dst, ssem, rsem, device):
        copy = pltpu.make_async_remote_copy(src_ref=src, dst_ref=dst, send_sem=ssem, recv_sem=rsem,
                                            device_id=device, device_id_type=MESH)
        copy.start()
        sends.append(copy)

    def arrived(dst, sem):
        pltpu.make_async_remote_copy(src_ref=dst, dst_ref=dst, send_sem=sem, recv_sem=sem,
                                     device_id=sibling, device_id_type=MESH).wait_recv()

    own = pltpu.make_async_copy(features, xbuf.at[0], loc.at[0])
    own.start()
    barrier = pltpu.get_barrier_semaphore()
    partners = [at_z(d) for d in RING8] + [at_x(d) for d in RING4] + [at_y(d) for d in RING8] + [sibling]
    for device in partners:
        pl.semaphore_signal(barrier, inc=1, device_id=device, device_id_type=MESH)
    part = tiles.shape[0] // 4
    edge = [pltpu.make_async_copy(tiles.at[pl.ds(i * part, part)], tile_buf.at[pl.ds(i * part, part)], loc.at[1 + i])
            for i in range(4)]
    wcopy = pltpu.make_async_copy(weight, wbuf, loc.at[5])
    ccopy = pltpu.make_async_copy(cotangent, cbuf, loc.at[6])
    small = [pltpu.make_async_copy(a, b, loc.at[9 + i]) for i, (a, b) in enumerate(
        ((tile_row, rows_v), (tile_col, cols_v), (labels, labels_v)))]
    for copy in small + edge + [wcopy, ccopy]:
        copy.start()
    own.wait()
    pl.semaphore_wait(barrier, len(partners))

    for dz in (1, 7, 2, 6, 3, 5, 4):
        push(xbuf.at[0], xbuf.at[dz], ag_s.at[dz], ag_r.at[dz], at_z(dz))
    for dx in RING4:
        push(xbuf.at[0], xbuf.at[dx * NZ], ag_s.at[dx * NZ], ag_r.at[dx * NZ], at_x(dx))
    for dz in (1, 7, 2, 6, 3, 5, 4):
        arrived(xbuf.at[dz], ag_r.at[dz])
        for dx in RING4:
            s = dx * NZ + dz
            push(xbuf.at[dz], xbuf.at[s], ag_s.at[s], ag_r.at[s], at_x(dx))
    for copy in small:
        copy.wait()
    slots[...] = jnp.zeros_like(slots)
    plan_v[...] = jnp.zeros_like(plan_v)
    slots[0:1, 0:tile_row.shape[1]] = rows_v[...]
    slots[1:2, 0:tile_row.shape[1]] = cols_v[...]
    rows_here, cols_here = slots[0:1, :], slots[1:2, :]
    live = iota((1, WIDE), 1) < tile_count[0, 0]
    xbuf[NX * NZ] = jnp.zeros((T, T), BF)
    for h in range(2):
        gbuf[h][NY * 2] = jnp.zeros((HALF, T), BF)
    to_row = ((rows_here // 2 - y + NY) % NY) * 2 + (rows_here + k) % 2
    from_row = ((y - rows_here // 2 + NY) % NY) * 2 + (rows_here + k) % 2
    to_col = ((cols_here // NZ - x + NX) % NX) * NZ + (cols_here - z + NZ) % NZ
    from_col = ((x - cols_here // NZ + NX) % NX) * NZ + (z - cols_here + 4 * NZ) % NZ
    make_plan(to_row, from_col, live, NX * NZ, plan_v.at[0])
    make_plan(to_col, from_row, live, NY * 2, plan_v.at[1])
    fcopy = pltpu.make_async_copy(plan_v.at[0], plan_f, loc.at[7])
    bcopy = pltpu.make_async_copy(plan_v.at[1], plan_b, loc.at[8])
    fcopy.start()
    bcopy.start()

    for copy in edge + [wcopy, ccopy, fcopy, bcopy]:
        copy.wait()
    for dz in (0, 1, 7, 2, 6, 3, 5, 4):
        for dx in (1, 3, 2):
            arrived(xbuf.at[dx * NZ + dz], ag_r.at[dx * NZ + dz])

    def within(index, size):
        return jnp.minimum(jnp.maximum(index, 0), size - 1)

    def run(plan, pairs, unroll, blocks, sums, product):
        def body(step, total):
            for u in range(unroll):
                pair = step * unroll + u
                first, second = 2 * pair, 2 * pair + 1
                value = product(
                    within(plan[0, first], tile_buf.shape[0]), within(plan[0, second], tile_buf.shape[0]),
                    within(plan[1, first], blocks), within(plan[1, second], blocks))
                total = jnp.where(plan[2, first] > 0, total, 0.0) + value
                sums[pair] = total
            return total

        lax.fori_loop(0, pairs // unroll, body, jnp.zeros(sums.shape[1:], F32))

    def result(plan, group, sums):
        return jnp.where(plan[4, group] > 0, sums[within(plan[3, group], sums.shape[0])], 0.0).astype(BF)

    def forward(s0, s1, b0, b1):
        return mm(jnp.concatenate([tile_buf[s0], tile_buf[s1]], axis=1),
                  jnp.concatenate([xbuf[b0], xbuf[b1]], axis=0))

    def backward(h):
        def product(s0, s1, b0, b1):
            return mm(jnp.concatenate([gbuf[h][b0], gbuf[h][b1]], axis=1),
                      jnp.concatenate([tile_buf[s0], tile_buf[s1]], axis=0))
        return product

    slots_all = tiles.shape[0]
    run(plan_f, (slots_all + NY * 2) // 2, FORWARD_STEP, xbuf.shape[0], pref, forward)

    for ey in RING8 + (0,):
        pblk[ey * 2 + 1] = result(plan_f, ey * 2 + 1, pref)
        push(pblk.at[ey * 2 + 1], cr.at[ey], c_s.at[ey], c_r.at[ey], sibling)
    for ey in RING8 + (0,):
        pblk[ey * 2] = result(plan_f, ey * 2, pref)
    for ey in RING8:
        arrived(cr.at[ey], c_r.at[ey])
        ystage[ey] = (pblk[ey * 2].astype(F32) + cr[ey].astype(F32)).astype(BF)
        push(ystage.at[ey], yr.at[ey], y_s.at[ey], y_r.at[ey], at_y(ey))
    arrived(cr.at[0], c_r.at[0])
    total = pblk[0].astype(F32) + cr[0].astype(F32)
    diagonal = jnp.where(iota((T, T), 0) == iota((T, T), 1), jnp.where(labels_v[...] >= 0, 1.0, 0.0), 0.0).astype(BF)
    masked = cbuf[...].astype(F32) * mm(diagonal, jnp.ones((T, WIDE), BF))
    for ey in (1, 7, 2, 6, 3, 5, 4):
        arrived(yr.at[ey], y_r.at[ey])
        total = total + yr[ey].astype(F32)
    aggregate = total.astype(BF)
    preact = mm(aggregate, wbuf[...])
    sigmoid_v = jax.nn.sigmoid(preact)
    grad_pre = (masked * sigmoid_v * (1.0 + preact * (1.0 - sigmoid_v))).astype(BF)
    projected = mm_t(wbuf[...], grad_pre).astype(BF)
    gbuf[0][0] = projected[:HALF]
    gbuf[1][0] = projected[HALF:]

    for h in range(2):
        for dy in (1, 7, 2, 6, 3, 5, 4):
            push(gbuf[h].at[0], gbuf[h].at[dy * 2], g_s.at[h, dy * 2], g_r.at[h, dy * 2], at_y(dy))
        push(gbuf[h].at[0], gbuf[h].at[1], g_s.at[h, 1], g_r.at[h, 1], sibling)
    act_out[...] = (preact * sigmoid_v).astype(BF)
    wt[...] = lax.dot_general(aggregate, grad_pre, (((0,), (0,)), ((), ())), preferred_element_type=F32)
    half = T // 2
    mine = pl.ds(pl.multiple_of(k * half, half), half)
    theirs = pl.ds(pl.multiple_of(other * half, half), half)
    push(wt.at[theirs], w0r, w_s.at[0], w0_r, sibling)
    arrived(w0r, w0_r)
    wh[...] = wt[mine, :] + w0r[...]
    piece = half // NY

    def rows_of(d):
        return pl.ds(pl.multiple_of(((y + d) % NY) * piece, piece), piece)

    for ey in RING8:
        push(wh.at[rows_of(ey)], w1r.at[ey], w_s.at[ey], w1_r.at[ey], at_y(ey))
    def hand_on(h):
        for dy in (1, 7, 2, 6, 3, 5, 4):
            arrived(gbuf[h].at[dy * 2], g_r.at[h, dy * 2])
            push(gbuf[h].at[dy * 2], gbuf[h].at[dy * 2 + 1], g_s.at[h, dy * 2 + 1], g_r.at[h, dy * 2 + 1], sibling)

    def transposed_sums(h):
        for dy in (0, 1, 7, 2, 6, 3, 5, 4):
            arrived(gbuf[h].at[dy * 2 + 1], g_r.at[h, dy * 2 + 1])
        run(plan_b, (slots_all + NX * NZ) // 2, BACKWARD_STEP, gbuf[h].shape[0], pref2.at[h], backward(h))

    def send_x(h):
        for ez in RING8 + (0,):
            for ex in RING4:
                g = ex * NZ + ez
                bblk[h, g] = result(plan_b, g, pref2.at[h])
                push(bblk.at[h, g], xr.at[h, g], x_s.at[h, g], x_r.at[h, g], at_x(ex))
        for ez in range(NZ):
            bblk[h, ez] = result(plan_b, ez, pref2.at[h])

    hand_on(0)
    transposed_sums(0)
    hand_on(1)
    term = wh[rows_of(0), :]
    for ey in RING8:
        arrived(w1r.at[ey], w1_r.at[ey])
        term = term + w1r[ey]
    w2b[x] = term
    for dx in RING4:
        push(w2b.at[x], w2b.at[x], w_s.at[8 + dx], w2_r.at[dx], at_x(dx))

    send_x(0)
    transposed_sums(1)
    send_x(1)
    for dx in RING4:
        arrived(w2b.at[(x + NX - dx) % NX], w2_r.at[dx])
    term = w2b[0]
    for i in range(1, NX):
        term = term + w2b[i]
    w3b[z] = term
    for dz in RING8:
        push(w3b.at[z], w3b.at[z], w_s.at[12 + dz], w3_r.at[dz], at_z(dz))

    def x_total(h, ez):
        total = bblk[h, ez].astype(F32)
        for ex in (1, 3, 2):
            g = ex * NZ + ez
            arrived(xr.at[h, g], x_r.at[h, g])
            total = total + xr[h, g].astype(F32)
        return total

    def gw_rows(d):
        return pl.ds(pl.multiple_of(k * half + ((y + NY + d) % NY) * piece, piece), piece)

    def send_z(h):
        for ez in RING8:
            zstage[h, ez] = x_total(h, ez).astype(BF)
            push(zstage.at[h, ez], zr.at[h, ez], z_s.at[h, ez], z_r.at[h, ez], at_z(ez))

    send_z(0)
    for dz in RING8:
        arrived(w3b.at[(z + NZ - dz) % NZ], w3_r.at[dz])
    term = w3b[0]
    for i in range(1, NZ):
        term = term + w3b[i]
    gw_out[gw_rows(0), :] = term * (float(T * NX * NZ * NY * 2) ** -0.5)
    for dy in RING8:
        push(gw_out.at[gw_rows(0)], gw_out.at[gw_rows(0)], w_s.at[20 + dy], w4_r.at[dy], at_y(dy))
    total_a = x_total(0, 0)
    send_z(1)
    total_b = x_total(1, 0)
    for dy in RING8:
        arrived(gw_out.at[gw_rows(-dy)], w4_r.at[dy])
    push(gw_out.at[mine], gw_out.at[mine], w_s.at[28], w5_r, sibling)
    for ez in (1, 7, 2, 6, 3, 5, 4):
        arrived(zr.at[0, ez], z_r.at[0, ez])
        total_a = total_a + zr[0, ez].astype(F32)
    for ez in (1, 7, 2, 6, 3, 5, 4):
        arrived(zr.at[1, ez], z_r.at[1, ez])
        total_b = total_b + zr[1, ez].astype(F32)
    gf_out[...] = jnp.transpose(jnp.concatenate([total_a, total_b], axis=0)).astype(BF)
    arrived(gw_out.at[theirs], w5_r)
    for copy in sends:
        copy.wait_send()


def shards(features, weight, edge_tiles, tile_row, tile_col, tile_count, labels, cotangent):
    count = edge_tiles.shape[2]
    nodes, width = features.shape
    hidden = weight.shape[1]
    pairs = (count + NX * NZ) // 2
    dma = pltpu.SemaphoreType.DMA
    hbm = pl.BlockSpec(memory_space=pltpu.HBM)
    vmem = pl.BlockSpec(memory_space=pltpu.VMEM)
    V = pltpu.VMEM
    return pl.pallas_call(
        kernel,
        out_shape=(
            jax.ShapeDtypeStruct((nodes, hidden), BF),
            jax.ShapeDtypeStruct((nodes, width), BF),
            jax.ShapeDtypeStruct((width, hidden), F32),
        ),
        in_specs=[hbm] * 7 + [pl.BlockSpec(memory_space=pltpu.SMEM)],
        out_specs=(vmem, vmem, vmem),
        scratch_shapes=[
            V((count, T, T), BF),
            V((NX * NZ + 1, T, T), BF),
            V((NY * 2 + 1, HALF, T), BF),
            V((NY * 2 + 1, HALF, T), BF),
            V(((count + NY * 2) // 2, T, T), F32),
            V((2, pairs, HALF, T), F32),
            V((NY * 2, T, T), BF),
            V((NY, T, T), BF),
            V((NY, T, T), BF),
            V((NY, T, T), BF),
            V((2, NX * NZ, HALF, T), BF),
            V((2, NX * NZ, HALF, T), BF),
            V((2, NZ, HALF, T), BF),
            V((2, NZ, HALF, T), BF),
            V((width, hidden), BF),
            V((nodes, hidden), BF),
            V((8, WIDE), I32),
            V((2, 8, WIDE), I32),
            pltpu.SMEM((8, WIDE), I32),
            pltpu.SMEM((8, WIDE), I32),
            V((width, hidden), F32),
            V((width // 2, hidden), F32),
            V((width // 2, hidden), F32),
            V((NY, width // 2 // NY, hidden), F32),
            V((NX, width // 2 // NY, hidden), F32),
            V((NZ, width // 2 // NY, hidden), F32),
            V((1, count), I32), V((1, count), I32), V((1, nodes), I32),
            dma((13,)),
            dma((NX * NZ,)), dma((NX * NZ,)),
            dma((NY,)), dma((NY,)),
            dma((NY,)), dma((NY,)),
            dma((2, NY * 2)), dma((2, NY * 2)),
            dma((2, NX * NZ)), dma((2, NX * NZ)),
            dma((2, NZ)), dma((2, NZ)),
            dma((30,)),
            dma, dma((NY,)), dma((NX,)), dma((NZ,)), dma((NY,)), dma,
        ],
        compiler_params=pltpu.CompilerParams(
            collective_id=0, has_side_effects=True, vmem_limit_bytes=40 * 1024 * 1024
        ),
    )(*(pltpu.with_memory_space_constraint(a, pltpu.HBM) for a in (
        features, weight, edge_tiles.reshape(count, T, T), tile_row.reshape(1, count), tile_col.reshape(1, count),
        labels.reshape(1, nodes), cotangent)), tile_count)


def solution(mesh):
    return jax.shard_map(
        shards,
        mesh=mesh,
        in_specs=(
            P(("row", "col"), None),
            P(),
            P("row", "col", None, None, None),
            P("row", "col", None),
            P("row", "col", None),
            P("row", "col"),
            P(("row", "col")),
            P(("row", "col"), None),
        ),
        out_specs=(P(("row", "col"), None), P(("row", "col"), None), P()),
        check_vma=False,
    )
```

```python
import jax
import jax.numpy as jnp
from jax import lax
from jax.experimental import pallas as pl
from jax.experimental.pallas import tpu as pltpu
from jax.sharding import PartitionSpec as P

MESH = pl.DeviceIdType.MESH
NX, NZ, NY = 4, 8, 8
T = 128
WIDE = 256
RING8 = (4, 3, 5, 2, 6, 1, 7)
RING4 = (2, 1, 3)
FORWARD_STEP, BACKWARD_STEP = 20, 22
PARTS = (48, 80)
BF, F32, I32 = jnp.bfloat16, jnp.float32, jnp.int32


def iota(shape, dim):
    return lax.broadcasted_iota(I32, shape, dim)


def mm(a, b):
    return jnp.dot(a, b, preferred_element_type=F32)


def mm_t(a, b):
    return lax.dot_general(a, b, (((1,), (1,)), ((), ())), preferred_element_type=F32)


def one_hot(mask):
    return jnp.where(mask, 1.0, 0.0).astype(BF)


def make_plan(keys, others, live, empty, out):
    groups = one_hot((iota((T, WIDE), 0) == keys) & live)
    before = one_hot(iota((WIDE, WIDE), 0) < iota((WIDE, WIDE), 1))
    rank = mm(groups, before)
    count = mm(groups, jnp.ones((WIDE, T), BF))
    padded = 2.0 * jnp.floor((count + 1.0) * 0.5)
    lower = one_hot(iota((T, T), 1) < iota((T, T), 0))
    start = mm(lower, padded.astype(BF))
    hot = groups.astype(F32)
    rank_here = jnp.sum(hot * rank, axis=0, keepdims=True)
    place = rank_here + jnp.sum(hot * start[:, :1], axis=0, keepdims=True)
    chosen = one_hot((iota((WIDE, WIDE), 0) == place.astype(I32)) & live)
    which = iota((8, WIDE), 0)
    slot = iota((8, WIDE), 1).astype(F32)
    rows = jnp.where(which == 0, slot, jnp.where(which == 1, others.astype(F32), jnp.where(
        which == 2, jnp.where(rank_here == 0.0, 1.0, 0.0), 1.0)))
    sorted_rows = mm_t(rows.astype(BF), chosen)
    count_row = mm_t(jnp.ones((8, WIDE), BF), groups)
    padded_row = 2.0 * jnp.floor((count_row + 1.0) * 0.5)
    upper = one_hot(iota((T, T), 0) < iota((T, T), 1))
    end_row = mm(padded_row.astype(BF), upper) + padded_row
    last_row = jnp.maximum(end_row * 0.5 - 1.0, 0.0)
    valid = sorted_rows[3:4] > 0.5
    out[0:1, :] = sorted_rows[0:1].astype(I32)
    out[1:2, :] = jnp.where(valid, sorted_rows[1:2], float(empty)).astype(I32)
    out[2:3, :] = (1.0 - sorted_rows[2:3]).astype(I32)
    out[3:4, 0:T] = last_row[0:1].astype(I32)
    out[4:5, 0:T] = jnp.where(count_row[0:1] > 0.5, 1.0, 0.0).astype(I32)


def kernel(features, weight, tiles, tile_row, tile_col, labels, cotangent, tile_count,
           act_out, gf_out, gw_out,
           tile_buf, xbuf, gbuf_a, gbuf_b, pref, pref_a, pref_b, pblk, cr, ystage, yr, bblk_a, bblk_b, xr_a, xr_b,
           zstage_a, zstage_b, zr_a, zr_b, wbuf, cbuf, slots,
           plan_v, plan_f, plan_b, wt, w0r, wh, w1r, w2b, w3b, rows_v, cols_v, labels_v,
           loc, ag_s, ag_r, c_s, c_r, y_s, y_r, g_s, g_r, x_s, x_r, z_s, z_r,
           w_s, w0_r, w1_r, w2_r, w3_r, w4_r, w5_r):
    r, c = lax.axis_index("row"), lax.axis_index("col")
    gbuf, pref2, bblk = (gbuf_a, gbuf_b), (pref_a, pref_b), (bblk_a, bblk_b)
    xr, zstage, zr = (xr_a, xr_b), (zstage_a, zstage_b), (zr_a, zr_b)
    x, z, y, k = r // NZ, r % NZ, c // 2, c % 2
    other = 1 - k

    def at_x(d):
        return (((x + d) % NX) * NZ + z, c)

    def at_z(d):
        return (x * NZ + (z + d) % NZ, c)

    def at_y(d):
        return (r, ((y + d) % NY) * 2 + k)

    sibling = (r, y * 2 + other)
    sends = []

    def push(src, dst, ssem, rsem, device):
        copy = pltpu.make_async_remote_copy(src_ref=src, dst_ref=dst, send_sem=ssem, recv_sem=rsem,
                                            device_id=device, device_id_type=MESH)
        copy.start()
        sends.append(copy)

    def arrived(dst, sem):
        pltpu.make_async_remote_copy(src_ref=dst, dst_ref=dst, send_sem=sem, recv_sem=sem,
                                     device_id=sibling, device_id_type=MESH).wait_recv()

    own = pltpu.make_async_copy(features, xbuf.at[0], loc.at[0])
    own.start()
    barrier = pltpu.get_barrier_semaphore()
    partners = [at_z(d) for d in RING8] + [at_x(d) for d in RING4] + [at_y(d) for d in RING8] + [sibling]
    for device in partners:
        pl.semaphore_signal(barrier, inc=1, device_id=device, device_id_type=MESH)
    part = tiles.shape[0] // 4
    edge = [pltpu.make_async_copy(tiles.at[pl.ds(i * part, part)], tile_buf.at[pl.ds(i * part, part)], loc.at[1 + i])
            for i in range(4)]
    wcopy = pltpu.make_async_copy(weight, wbuf, loc.at[5])
    ccopy = pltpu.make_async_copy(cotangent, cbuf, loc.at[6])
    small = [pltpu.make_async_copy(a, b, loc.at[9 + i]) for i, (a, b) in enumerate(
        ((tile_row, rows_v), (tile_col, cols_v), (labels, labels_v)))]
    for copy in small + edge + [wcopy, ccopy]:
        copy.start()
    own.wait()
    pl.semaphore_wait(barrier, len(partners))

    for dz in (1, 7, 2, 6, 3, 5, 4):
        push(xbuf.at[0], xbuf.at[dz], ag_s.at[dz], ag_r.at[dz], at_z(dz))
    for dx in RING4:
        push(xbuf.at[0], xbuf.at[dx * NZ], ag_s.at[dx * NZ], ag_r.at[dx * NZ], at_x(dx))
    for dz in (1, 7, 2, 6, 3, 5, 4):
        arrived(xbuf.at[dz], ag_r.at[dz])
        for dx in RING4:
            s = dx * NZ + dz
            push(xbuf.at[dz], xbuf.at[s], ag_s.at[s], ag_r.at[s], at_x(dx))
    for copy in small:
        copy.wait()
    slots[...] = jnp.zeros_like(slots)
    plan_v[...] = jnp.zeros_like(plan_v)
    slots[0:1, 0:tile_row.shape[1]] = rows_v[...]
    slots[1:2, 0:tile_row.shape[1]] = cols_v[...]
    rows_here, cols_here = slots[0:1, :], slots[1:2, :]
    live = iota((1, WIDE), 1) < tile_count[0, 0]
    xbuf[NX * NZ] = jnp.zeros((T, T), BF)
    for h in range(2):
        gbuf[h][NY * 2] = jnp.zeros((PARTS[h], T), BF)
    to_row = ((rows_here // 2 - y + NY) % NY) * 2 + (rows_here + k) % 2
    from_row = ((y - rows_here // 2 + NY) % NY) * 2 + (rows_here + k) % 2
    to_col = ((cols_here // NZ - x + NX) % NX) * NZ + (cols_here - z + NZ) % NZ
    from_col = ((x - cols_here // NZ + NX) % NX) * NZ + (z - cols_here + 4 * NZ) % NZ
    make_plan(to_row, from_col, live, NX * NZ, plan_v.at[0])
    make_plan(to_col, from_row, live, NY * 2, plan_v.at[1])
    fcopy = pltpu.make_async_copy(plan_v.at[0], plan_f, loc.at[7])
    bcopy = pltpu.make_async_copy(plan_v.at[1], plan_b, loc.at[8])
    fcopy.start()
    bcopy.start()

    for copy in edge + [wcopy, ccopy, fcopy, bcopy]:
        copy.wait()
    for dz in (0, 1, 7, 2, 6, 3, 5, 4):
        for dx in (1, 3, 2):
            arrived(xbuf.at[dx * NZ + dz], ag_r.at[dx * NZ + dz])

    def within(index, size):
        return jnp.minimum(jnp.maximum(index, 0), size - 1)

    def run(plan, pairs, unroll, blocks, sums, product):
        def body(step, total):
            for u in range(unroll):
                pair = step * unroll + u
                first, second = 2 * pair, 2 * pair + 1
                value = product(
                    within(plan[0, first], tile_buf.shape[0]), within(plan[0, second], tile_buf.shape[0]),
                    within(plan[1, first], blocks), within(plan[1, second], blocks))
                total = jnp.where(plan[2, first] > 0, total, 0.0) + value
                sums[pair] = total
            return total

        lax.fori_loop(0, pairs // unroll, body, jnp.zeros(sums.shape[1:], F32))

    def result(plan, group, sums):
        return jnp.where(plan[4, group] > 0, sums[within(plan[3, group], sums.shape[0])], 0.0).astype(BF)

    def forward(s0, s1, b0, b1):
        return mm(jnp.concatenate([tile_buf[s0], tile_buf[s1]], axis=1),
                  jnp.concatenate([xbuf[b0], xbuf[b1]], axis=0))

    def backward(h):
        def product(s0, s1, b0, b1):
            return mm(jnp.concatenate([gbuf[h][b0], gbuf[h][b1]], axis=1),
                      jnp.concatenate([tile_buf[s0], tile_buf[s1]], axis=0))
        return product

    slots_all = tiles.shape[0]
    run(plan_f, (slots_all + NY * 2) // 2, FORWARD_STEP, xbuf.shape[0], pref, forward)

    for ey in RING8 + (0,):
        pblk[ey * 2 + 1] = result(plan_f, ey * 2 + 1, pref)
        push(pblk.at[ey * 2 + 1], cr.at[ey], c_s.at[ey], c_r.at[ey], sibling)
    for ey in RING8 + (0,):
        pblk[ey * 2] = result(plan_f, ey * 2, pref)
    for ey in RING8:
        arrived(cr.at[ey], c_r.at[ey])
        ystage[ey] = (pblk[ey * 2].astype(F32) + cr[ey].astype(F32)).astype(BF)
        push(ystage.at[ey], yr.at[ey], y_s.at[ey], y_r.at[ey], at_y(ey))
    arrived(cr.at[0], c_r.at[0])
    total = pblk[0].astype(F32) + cr[0].astype(F32)
    diagonal = jnp.where(iota((T, T), 0) == iota((T, T), 1), jnp.where(labels_v[...] >= 0, 1.0, 0.0), 0.0).astype(BF)
    masked = cbuf[...].astype(F32) * mm(diagonal, jnp.ones((T, WIDE), BF))
    for ey in (1, 7, 2, 6, 3, 5, 4):
        arrived(yr.at[ey], y_r.at[ey])
        total = total + yr[ey].astype(F32)
    aggregate = total.astype(BF)
    preact = mm(aggregate, wbuf[...])
    sigmoid_v = jax.nn.sigmoid(preact)
    grad_pre = (masked * sigmoid_v * (1.0 + preact * (1.0 - sigmoid_v))).astype(BF)
    projected = mm_t(wbuf[...], grad_pre).astype(BF)
    gbuf[0][0] = projected[:PARTS[0]]
    gbuf[1][0] = projected[PARTS[0]:]

    def send_y(h):
        for dy in (1, 7, 2, 6, 3, 5, 4):
            push(gbuf[h].at[0], gbuf[h].at[dy * 2], g_s.at[h, dy * 2], g_r.at[h, dy * 2], at_y(dy))
        push(gbuf[h].at[0], gbuf[h].at[1], g_s.at[h, 1], g_r.at[h, 1], sibling)

    send_y(0)
    wt[...] = lax.dot_general(aggregate, grad_pre, (((0,), (0,)), ((), ())), preferred_element_type=F32)
    half = T // 2
    mine = pl.ds(pl.multiple_of(k * half, half), half)
    theirs = pl.ds(pl.multiple_of(other * half, half), half)
    push(wt.at[theirs], w0r, w_s.at[0], w0_r, sibling)
    arrived(w0r, w0_r)
    wh[...] = wt[mine, :] + w0r[...]
    piece = half // NY

    def rows_of(d):
        return pl.ds(pl.multiple_of(((y + d) % NY) * piece, piece), piece)

    for ey in RING8:
        push(wh.at[rows_of(ey)], w1r.at[ey], w_s.at[ey], w1_r.at[ey], at_y(ey))
    send_y(1)
    act_out[...] = (preact * sigmoid_v).astype(BF)

    def hand_on(h):
        for dy in (1, 7, 2, 6, 3, 5, 4):
            arrived(gbuf[h].at[dy * 2], g_r.at[h, dy * 2])
            push(gbuf[h].at[dy * 2], gbuf[h].at[dy * 2 + 1], g_s.at[h, dy * 2 + 1], g_r.at[h, dy * 2 + 1], sibling)

    def transposed_sums(h):
        for dy in (0, 1, 7, 2, 6, 3, 5, 4):
            arrived(gbuf[h].at[dy * 2 + 1], g_r.at[h, dy * 2 + 1])
        run(plan_b, (slots_all + NX * NZ) // 2, BACKWARD_STEP, gbuf[h].shape[0], pref2[h], backward(h))

    def send_x(h):
        for ez in RING8 + (0,):
            for ex in RING4:
                g = ex * NZ + ez
                bblk[h][g] = result(plan_b, g, pref2[h])
                push(bblk[h].at[g], xr[h].at[g], x_s.at[h, g], x_r.at[h, g], at_x(ex))
        for ez in range(NZ):
            bblk[h][ez] = result(plan_b, ez, pref2[h])

    hand_on(0)
    transposed_sums(0)
    hand_on(1)
    term = wh[rows_of(0), :]
    for ey in RING8:
        arrived(w1r.at[ey], w1_r.at[ey])
        term = term + w1r[ey]
    w2b[x] = term
    for dx in RING4:
        push(w2b.at[x], w2b.at[x], w_s.at[8 + dx], w2_r.at[dx], at_x(dx))

    send_x(0)
    transposed_sums(1)
    for dx in RING4:
        arrived(w2b.at[(x + NX - dx) % NX], w2_r.at[dx])
    term = w2b[0]
    for i in range(1, NX):
        term = term + w2b[i]
    w3b[z] = term
    for dz in RING8:
        push(w3b.at[z], w3b.at[z], w_s.at[12 + dz], w3_r.at[dz], at_z(dz))
    send_x(1)

    def x_total(h, ez):
        total = bblk[h][ez].astype(F32)
        for ex in (1, 3, 2):
            g = ex * NZ + ez
            arrived(xr[h].at[g], x_r.at[h, g])
            total = total + xr[h][g].astype(F32)
        return total

    def gw_rows(d):
        return pl.ds(pl.multiple_of(k * half + ((y + NY + d) % NY) * piece, piece), piece)

    def send_z(h):
        for ez in RING8:
            zstage[h][ez] = x_total(h, ez).astype(BF)
            push(zstage[h].at[ez], zr[h].at[ez], z_s.at[h, ez], z_r.at[h, ez], at_z(ez))

    send_z(0)
    for dz in RING8:
        arrived(w3b.at[(z + NZ - dz) % NZ], w3_r.at[dz])
    term = w3b[0]
    for i in range(1, NZ):
        term = term + w3b[i]
    gw_out[gw_rows(0), :] = term * (float(T * NX * NZ * NY * 2) ** -0.5)
    for dy in RING8:
        push(gw_out.at[gw_rows(0)], gw_out.at[gw_rows(0)], w_s.at[20 + dy], w4_r.at[dy], at_y(dy))
    total_a = x_total(0, 0)
    send_z(1)
    total_b = x_total(1, 0)
    for dy in RING8:
        arrived(gw_out.at[gw_rows(-dy)], w4_r.at[dy])
    push(gw_out.at[mine], gw_out.at[mine], w_s.at[28], w5_r, sibling)
    for ez in (1, 7, 2, 6, 3, 5, 4):
        arrived(zr[0].at[ez], z_r.at[0, ez])
        total_a = total_a + zr[0][ez].astype(F32)
    for ez in (1, 7, 2, 6, 3, 5, 4):
        arrived(zr[1].at[ez], z_r.at[1, ez])
        total_b = total_b + zr[1][ez].astype(F32)
    gf_out[...] = jnp.transpose(jnp.concatenate([total_a, total_b], axis=0)).astype(BF)
    arrived(gw_out.at[theirs], w5_r)
    for copy in sends:
        copy.wait_send()


def shards(features, weight, edge_tiles, tile_row, tile_col, tile_count, labels, cotangent):
    count = edge_tiles.shape[2]
    nodes, width = features.shape
    hidden = weight.shape[1]
    pairs = (count + NX * NZ) // 2
    dma = pltpu.SemaphoreType.DMA
    hbm = pl.BlockSpec(memory_space=pltpu.HBM)
    vmem = pl.BlockSpec(memory_space=pltpu.VMEM)
    V = pltpu.VMEM
    return pl.pallas_call(
        kernel,
        out_shape=(
            jax.ShapeDtypeStruct((nodes, hidden), BF),
            jax.ShapeDtypeStruct((nodes, width), BF),
            jax.ShapeDtypeStruct((width, hidden), F32),
        ),
        in_specs=[hbm] * 7 + [pl.BlockSpec(memory_space=pltpu.SMEM)],
        out_specs=(vmem, vmem, vmem),
        scratch_shapes=[
            V((count, T, T), BF),
            V((NX * NZ + 1, T, T), BF),
            *[V((NY * 2 + 1, p, T), BF) for p in PARTS],
            V(((count + NY * 2) // 2, T, T), F32),
            *[V((pairs, p, T), F32) for p in PARTS],
            V((NY * 2, T, T), BF),
            V((NY, T, T), BF),
            V((NY, T, T), BF),
            V((NY, T, T), BF),
            *[V((NX * NZ, p, T), BF) for p in PARTS],
            *[V((NX * NZ, p, T), BF) for p in PARTS],
            *[V((NZ, p, T), BF) for p in PARTS],
            *[V((NZ, p, T), BF) for p in PARTS],
            V((width, hidden), BF),
            V((nodes, hidden), BF),
            V((8, WIDE), I32),
            V((2, 8, WIDE), I32),
            pltpu.SMEM((8, WIDE), I32),
            pltpu.SMEM((8, WIDE), I32),
            V((width, hidden), F32),
            V((width // 2, hidden), F32),
            V((width // 2, hidden), F32),
            V((NY, width // 2 // NY, hidden), F32),
            V((NX, width // 2 // NY, hidden), F32),
            V((NZ, width // 2 // NY, hidden), F32),
            V((1, count), I32), V((1, count), I32), V((1, nodes), I32),
            dma((13,)),
            dma((NX * NZ,)), dma((NX * NZ,)),
            dma((NY,)), dma((NY,)),
            dma((NY,)), dma((NY,)),
            dma((2, NY * 2)), dma((2, NY * 2)),
            dma((2, NX * NZ)), dma((2, NX * NZ)),
            dma((2, NZ)), dma((2, NZ)),
            dma((30,)),
            dma, dma((NY,)), dma((NX,)), dma((NZ,)), dma((NY,)), dma,
        ],
        compiler_params=pltpu.CompilerParams(
            collective_id=0, has_side_effects=True, vmem_limit_bytes=40 * 1024 * 1024
        ),
    )(*(pltpu.with_memory_space_constraint(a, pltpu.HBM) for a in (
        features, weight, edge_tiles.reshape(count, T, T), tile_row.reshape(1, count), tile_col.reshape(1, count),
        labels.reshape(1, nodes), cotangent)), tile_count)


def solution(mesh):
    return jax.shard_map(
        shards,
        mesh=mesh,
        in_specs=(
            P(("row", "col"), None),
            P(),
            P("row", "col", None, None, None),
            P("row", "col", None),
            P("row", "col", None),
            P("row", "col"),
            P(("row", "col")),
            P(("row", "col"), None),
        ),
        out_specs=(P(("row", "col"), None), P(("row", "col"), None), P()),
        check_vma=False,
    )
```
